256 devices in a mesh: dp: 8 (over y, z_lo), context: 32 (over x, z_hi, core).
Axes of the slice: x: 4, y: 4, z: 8 (z_hi: 4, z_lo: 2; z = z_hi * 2 + z_lo), core: 2. Of those that a mesh axis runs over, the one named last changes fastest.
Arguments:
- query_rows: bfloat16 [32768, 4096], P(('dp', 'context')), parts along dimension 0, may hold values from -6 to 6
- key_rows: bfloat16 [32768, 512], P(('dp', 'context')), parts along dimension 0, may hold values from -6 to 6
- value_rows: bfloat16 [32768, 512], P(('dp', 'context')), parts along dimension 0, may hold values from -6 to 6
- grad_out: bfloat16 [32768, 4096], P(('dp', 'context')), parts along dimension 0, may hold values from -6 to 6
- doc_bounds: int32 [72], P('dp'), parts along dimension 0, may hold values from 0 to 4096, as said below
Outputs:
- attn_out: bfloat16 [32768, 4096], P(('dp', 'context')), parts along dimension 0
- d_query: bfloat16 [32768, 4096], P(('dp', 'context')), parts along dimension 0
- d_key: bfloat16 [32768, 512], P(('dp', 'context')), parts along dimension 0
- d_value: bfloat16 [32768, 512], P(('dp', 'context')), parts along dimension 0
The draws below stay inside these ranges and needn't reach their ends.
There are 8 independent parts, one for each index of `dp`. The reference program is written for one: setup_inputs(seed, part) draws one part's arguments, and reference() takes and returns one part's arrays. A program takes and returns all parts, laid end to end along the dimension named above; each array names one. Nothing has to cross between parts.
Inputs may be any that keep to these rules, and one draw needn't show every extreme that they name: doc_bounds[0] = 0, doc_bounds[8] = 4096, strictly rising; every response is 256 to 1024 tokens long; at least one is exactly 1024 and at least one exactly 256.
All inputs are finite; a program needn't handle non-finite values.
Results may differ from the reference program's by a relative error of at most 0.035.
Values may be sent and summed in bfloat16 or wider, within the bound.
A program may use at most 64 MiB of HBM per device.

```python
import jax
import jax.numpy as jnp
from jax import lax

H = 32
KVH = 4
HEAD_DIM = 128
MINDOC = 256
MAXDOC = 1024
QBLOCK = 512
TOKENS = 4096
NDOC = 8


def draw_query_rows(key, part):
    key = jax.random.fold_in(key, 11)
    rows = jnp.clip(1.5 * jax.random.normal(key, (TOKENS, H * HEAD_DIM), jnp.float32), -6.0, 6.0)
    return rows.astype(jnp.bfloat16)


def draw_key_rows(key, part):
    key = jax.random.fold_in(key, 23)
    rows = jnp.clip(jax.random.normal(key, (TOKENS, KVH * HEAD_DIM), jnp.float32), -6.0, 6.0)
    return rows.astype(jnp.bfloat16)


def draw_doc_bounds(key, part):
    key = jax.random.fold_in(key, 7)
    key_pair, key_special, key_order = jax.random.split(key, 3)
    half_count = NDOC // 2
    offsets = jax.random.randint(key_pair, (half_count,), 0, 2 * MINDOC + 1)
    first = MINDOC + offsets
    second = 3 * MINDOC - offsets
    extra = jax.random.randint(key_special, (1,), 0, MINDOC + 1)
    special = jnp.concatenate([jnp.array([4 * MINDOC, MINDOC], jnp.int32), MINDOC + extra, 2 * MINDOC - extra])
    lengths = jnp.concatenate([special, first[2:], second[2:]]).astype(jnp.int32)
    lengths = lengths[jax.random.permutation(key_order, NDOC)]
    return jnp.concatenate([jnp.zeros((1,), jnp.int32), jnp.cumsum(lengths).astype(jnp.int32)])


def shard_levels(key, extent, shards, smallest, top_value):
    loudness, own = 1.0, jax.random.fold_in(key, 6)
    for dim, shards_of in shards:
        draws = jnp.exp(jax.random.uniform(jax.random.fold_in(own, dim), (shards_of,), jnp.float32, smallest / len(shards), top_value / len(shards)))
        loudness = loudness * jnp.repeat(draws, extent[dim] // shards_of).reshape([-1 if axis == dim else 1 for axis in range(len(extent))])
    return loudness


def normal_values(own_key, dims, scale, reach, shards=(), kind=jnp.bfloat16):
    gain = shard_levels(own_key, dims, shards, -0.22, 0.18) if shards else 1.0
    values = jax.random.normal(own_key, dims, jnp.float32) * scale * gain
    return jnp.minimum(jnp.maximum(values, -reach), reach).astype(kind)


def setup_inputs(seed: int = 0, part: int = 0) -> dict:
    key_of = jax.random.split(jax.random.key(seed), 6)
    own_keys = jax.random.split(jax.random.fold_in(key_of[5], part), 6)
    return {
        "query_rows": draw_query_rows(jax.random.fold_in(jax.random.fold_in(key_of[5], part), 71), part),
        "key_rows": draw_key_rows(jax.random.fold_in(jax.random.fold_in(key_of[5], part), 71), part),
        "value_rows": normal_values(own_keys[2], (TOKENS, KVH * HEAD_DIM), 1.0, 6.0, ((0, 32),)),
        "grad_out": normal_values(own_keys[3], (TOKENS, H * HEAD_DIM), 1.0, 6.0, ((0, 32),)),
        "doc_bounds": draw_doc_bounds(jax.random.fold_in(jax.random.fold_in(key_of[5], part), 71), part),
    }


masked_score = -1e30


def segment_ids(positions, doc_bounds):
    inner_bounds = doc_bounds[1:-1]
    return jnp.sum((positions[:, None] >= inner_bounds[None, :]).astype(jnp.int32), axis=1)


def block_pass(q_block, k_window, v_window, o_grad, allowed, softmax_scale):
    scores = jnp.einsum('qhd,kd->hqk', q_block.astype(jnp.float32), k_window.astype(jnp.float32)) * softmax_scale
    scores = jnp.where(allowed[None], scores, masked_score)
    top_score = jnp.max(scores, axis=-1, keepdims=True)
    expd = jnp.where(allowed[None], jnp.exp(scores - top_score), 0.0)
    probs = expd / jnp.sum(expd, axis=-1, keepdims=True)
    weights = probs.astype(jnp.bfloat16)
    attended = jnp.einsum('hqk,kd->qhd', weights.astype(jnp.float32), v_window.astype(jnp.float32)).astype(jnp.bfloat16)
    inner_prod = jnp.sum(o_grad.astype(jnp.float32) * attended.astype(jnp.float32), axis=-1)
    prob_grad = jnp.einsum('qhd,kd->hqk', o_grad.astype(jnp.float32), v_window.astype(jnp.float32))
    score_grad = (probs * (prob_grad - jnp.transpose(inner_prod)[:, :, None])).astype(jnp.bfloat16)
    q_grad = (softmax_scale * jnp.einsum('hqk,kd->qhd', score_grad.astype(jnp.float32), k_window.astype(jnp.float32))).astype(jnp.bfloat16)
    k_grad = softmax_scale * jnp.einsum('hqk,qhd->kd', score_grad.astype(jnp.float32), q_block.astype(jnp.float32))
    v_grad = jnp.einsum('hqk,qhd->kd', weights.astype(jnp.float32), o_grad.astype(jnp.float32))
    return attended, q_grad, k_grad, v_grad


def head_pass(q_heads, k_head, v_head, g_heads, doc_bounds, softmax_scale):
    length = q_heads.shape[0]
    width = k_head.shape[1]
    span = QBLOCK + MAXDOC
    k_pad = jnp.concatenate([jnp.zeros((MAXDOC, width), k_head.dtype), k_head], axis=0)
    v_pad = jnp.concatenate([jnp.zeros((MAXDOC, width), v_head.dtype), v_head], axis=0)
    seg_all = segment_ids(jnp.arange(length + MAXDOC, dtype=jnp.int32) - MAXDOC, doc_bounds)

    def step(carry, start):
        k_acc, v_acc = carry
        q_block = lax.dynamic_slice_in_dim(q_heads, start, QBLOCK, 0)
        g_block = lax.dynamic_slice_in_dim(g_heads, start, QBLOCK, 0)
        k_window = lax.dynamic_slice_in_dim(k_pad, start, span, 0)
        v_window = lax.dynamic_slice_in_dim(v_pad, start, span, 0)
        q_pos = start + jnp.arange(QBLOCK, dtype=jnp.int32)
        k_pos = start - MAXDOC + jnp.arange(span, dtype=jnp.int32)
        q_seg = lax.dynamic_slice_in_dim(seg_all, start + MAXDOC, QBLOCK, 0)
        k_seg = lax.dynamic_slice_in_dim(seg_all, start, span, 0)
        allowed = (q_seg[:, None] == k_seg[None, :]) & (k_pos[None, :] <= q_pos[:, None]) & (k_pos[None, :] >= 0)
        attended, q_grad, k_grad, v_grad = block_pass(q_block, k_window, v_window, g_block, allowed, softmax_scale)
        k_acc = lax.dynamic_update_slice_in_dim(k_acc, lax.dynamic_slice_in_dim(k_acc, start, span, 0) + k_grad, start, 0)
        v_acc = lax.dynamic_update_slice_in_dim(v_acc, lax.dynamic_slice_in_dim(v_acc, start, span, 0) + v_grad, start, 0)
        return (k_acc, v_acc), (attended, q_grad)

    starts = jnp.arange(0, length, QBLOCK, dtype=jnp.int32)
    empty = jnp.zeros((length + MAXDOC, width), jnp.float32)
    (k_acc, v_acc), (attended, q_grad) = lax.scan(step, (empty, empty), starts)
    heads_here = q_heads.shape[1]
    return (attended.reshape(length, heads_here, width), q_grad.reshape(length, heads_here, width),
            k_acc[MAXDOC:], v_acc[MAXDOC:])


def reference(query_rows, key_rows, value_rows, grad_out, doc_bounds):
    length = query_rows.shape[0]
    group = H // KVH
    softmax_scale = HEAD_DIM ** -0.5
    q_heads = query_rows.reshape(length, H, HEAD_DIM).transpose(1, 0, 2)
    g_heads = grad_out.reshape(length, H, HEAD_DIM).transpose(1, 0, 2)
    k_heads = key_rows.reshape(length, KVH, HEAD_DIM).transpose(1, 0, 2)
    v_heads = value_rows.reshape(length, KVH, HEAD_DIM).transpose(1, 0, 2)

    def one_head(inputs):
        q_one, g_one, head = inputs
        k_one = lax.dynamic_index_in_dim(k_heads, head // group, 0, keepdims=False)
        v_one = lax.dynamic_index_in_dim(v_heads, head // group, 0, keepdims=False)
        attended, q_grad, k_grad, v_grad = head_pass(q_one[:, None, :], k_one, v_one, g_one[:, None, :], doc_bounds, softmax_scale)
        return attended[:, 0], q_grad[:, 0], k_grad, v_grad

    attended, q_grad, k_grad, v_grad = lax.map(one_head, (q_heads, g_heads, jnp.arange(H, dtype=jnp.int32)))
    attn_out = attended.transpose(1, 0, 2).reshape(length, H * HEAD_DIM)
    d_query = q_grad.transpose(1, 0, 2).reshape(length, H * HEAD_DIM)
    d_key = k_grad.reshape(KVH, group, length, HEAD_DIM).sum(axis=1).transpose(1, 0, 2).reshape(length, KVH * HEAD_DIM)
    d_value = v_grad.reshape(KVH, group, length, HEAD_DIM).sum(axis=1).transpose(1, 0, 2).reshape(length, KVH * HEAD_DIM)
    return attn_out, d_query, d_key.astype(jnp.bfloat16), d_value.astype(jnp.bfloat16)
```

```python
import functools

import jax
import jax.numpy as jnp
from jax import lax
from jax.experimental import pallas as pl
from jax.experimental.pallas import tpu as pltpu
from jax.sharding import PartitionSpec as P

BF = jnp.bfloat16
F32 = jnp.float32
MESH = pl.DeviceIdType.MESH
MASKED = -1e30
SCALE = 128 ** -0.5
SCALE2 = SCALE * 1.4426950408889634
SLOTS = 3
CHIPS = 16
BACK = 4


def nt(a, b):
    return lax.dot_general(a, b, (((1,), (1,)), ((), ())), preferred_element_type=F32)


def nn(a, b):
    return jnp.dot(a, b, preferred_element_type=F32)


def in_doc(pos0, bounds):
    pos = lax.broadcasted_iota(jnp.int32, (128, 128), 0) + pos0
    lane = lax.broadcasted_iota(jnp.int32, (128, 128), 1)
    hit = jnp.zeros((128, 128), F32)
    for t in range(8):
        inside = (pos >= bounds[t]) & (pos < bounds[t + 1]) & (lane == t)
        hit = jnp.where(inside, 1.0, hit)
    return hit, lane < 8


def prep_masks(q0, bounds, ka, qa):
    for a in range(2):
        hit, _ = in_doc(q0 + a * 128, bounds)
        qa[a, 0:128, :] = hit.astype(BF)
        qa[a, 128:256, :] = hit.astype(BF)
    for j in range(10):
        hit, lanes = in_doc(q0 - 1024 + j * 128, bounds)
        ka[j * 128 : (j + 1) * 128, :] = jnp.where(lanes, (1.0 - hit) * MASKED, 0.0).astype(BF)


def prep_transposed(g, kv, kt, vt):
    for j in range(10):
        r = slice(j * 128, (j + 1) * 128)
        kt[g, :, r] = kv[g, 0, r, :].T
        vt[g, 0:128, r] = kv[g, 1, r, :].T


def pair(ref, a, h):
    return jnp.concatenate(
        [ref[a, :, h * 128 : h * 128 + 128], ref[a, :, h * 128 + 128 : h * 128 + 256]], axis=0
    )


def scores(g, i, qv, kv, ka, qa, s):
    a, hp = i // 4, i % 4
    q = jnp.concatenate([pair(qv, a, g * 8 + hp * 2), qa[a]], axis=1)
    m = jnp.full((8, 256), -3e38, F32)
    for kc in range(9):
        r = slice((a + kc) * 128, (a + kc + 1) * 128)
        sc = nt(jnp.concatenate([kv[g, 0, r, :], ka[r, :]], axis=1), q)
        if kc == 8:
            key = lax.broadcasted_iota(jnp.int32, (128, 256), 0)
            query = lax.broadcasted_iota(jnp.int32, (128, 256), 1) % 128
            sc = jnp.where(key <= query, sc, MASKED)
        s[i % SLOTS, kc * 128 : (kc + 1) * 128, :] = sc
        m = jnp.maximum(m, jnp.max(sc.reshape(16, 8, 256), axis=0))
    return jnp.max(m, axis=0, keepdims=True) * SCALE2


def exps(i, m, s, e):
    for kc in range(9):
        r = slice(kc * 128, (kc + 1) * 128)
        e[i, r, :] = jnp.exp2(s[i % SLOTS, r, :] * SCALE2 - m).astype(BF)


def attend(g, i, gv, vt, e, gs, dd, ov):
    a, hp = i // 4, i % 4
    h = g * 8 + hp * 2
    ot = nn(vt[g, :, a * 128 : a * 128 + 1152], e[i])
    o = ot[0:128].T
    linv = 1.0 / ot[128:136].T[:, 0:1]
    o = o * linv
    gp = (pair(gv, a, h).astype(F32) * linv).astype(BF)
    gs[i] = gp
    d = gp.astype(F32) * o
    dd[i] = jnp.broadcast_to(jnp.sum(d.T, axis=0, keepdims=True), (8, 256))
    ob = o.astype(BF)
    ov[a, :, h * 128 : h * 128 + 128] = ob[0:128]
    ov[a, :, h * 128 + 128 : h * 128 + 256] = ob[128:256]


def forward(g, qv, gv, kv, ka, qa, vt, s, e, gs, dd, ov):
    m = {}
    for t in range(10):
        if t < 8:
            m[t] = scores(g, t, qv, kv, ka, qa, s)
        if 1 <= t < 9:
            exps(t - 1, m[t - 1], s, e)
        if 2 <= t:
            attend(g, t - 2, gv, vt, e, gs, dd, ov)


def key_grads(g, kc, qv, kv, e, gs, dd, part):
    r = slice(kc * 128, (kc + 1) * 128)
    values = kv[g, 1, r, :]
    dk = jnp.zeros((128, 128), F32)
    dv = jnp.zeros((128, 128), F32)
    for a in range(2):
        if not 0 <= kc - a <= 8:
            continue
        rr = slice((kc - a) * 128, (kc - a + 1) * 128)
        for hp in range(4):
            i = a * 4 + hp
            dp = nt(values, gs[i])
            ei = e[i, rr, :]
            ds = ei * (dp - dd[i, 0:1, :]).astype(BF)
            e[i, rr, :] = ds
            dv = dv + nn(ei, gs[i])
            dk = dk + nn(ds, pair(qv, a, g * 8 + hp * 2))
    part[g, kc, 0] = (dk * SCALE).astype(BF)
    part[g, kc, 1] = dv.astype(BF)


def query_grads(g, i, kt, e, dqv):
    a, hp = i // 4, i % 4
    h = g * 8 + hp * 2
    dq = (nn(kt[g, :, a * 128 : a * 128 + 1152], e[i]) * SCALE).T.astype(BF)
    dqv[a, :, h * 128 : h * 128 + 128] = dq[0:128]
    dqv[a, :, h * 128 + 128 : h * 128 + 256] = dq[128:256]


def kernel(
    bounds, q_in, k_in, v_in, g_in,
    o_out, dq_out, dk_out, dv_out,
    qv, gv, kv, ka, qa, kt, vt, s, e, gs, dd, ov, dqv, part, got,
    own_sem, kv_own_sem, row_send, row_recv, kv_send, kv_recv, part_send, part_recv,
    out_own_sem, out_send, out_recv,
):
    dp = lax.axis_index("dp")
    c = lax.axis_index("context")
    chip, core = c // 2, c % 2
    other = 1 - core
    partner = chip * 2 + other

    def at(step, p):
        return lax.rem(chip + step + CHIPS, CHIPS) * 2 + p

    def cols(p, g, width):
        return pl.ds(pl.multiple_of(p * (2 * width) + g * width, width), width)

    def remote(src, dst, send, recv, to):
        return pltpu.make_async_remote_copy(
            src_ref=src, dst_ref=dst, send_sem=send, recv_sem=recv,
            device_id=(dp, to), device_id_type=MESH,
        )

    barrier = pltpu.get_barrier_semaphore()
    peers = [partner]
    for j in range(1, BACK + 1):
        for p in range(2):
            peers += [at(j, p), at(-j, p)]
    for peer in peers:
        pl.semaphore_signal(barrier, inc=1, device_id=(dp, peer), device_id_type=MESH)

    own = []
    for g in range(2):
        for n, (src, dst) in enumerate(((q_in, qv), (g_in, gv))):
            own.append(pltpu.make_async_copy(
                src.at[:, cols(core, g, 1024)], dst.at[core, :, g * 1024 : (g + 1) * 1024],
                own_sem.at[g, n]))
        for n, src in enumerate((k_in, v_in)):
            own.append(pltpu.make_async_copy(
                src.at[:, cols(core, g, 128)],
                kv.at[g, n, pl.ds(pl.multiple_of(1024 + core * 128, 128), 128)],
                kv_own_sem.at[g, n]))
    for copy in own:
        copy.start()
    pl.semaphore_wait(barrier, len(peers))

    def row_copy(g, n, src, dst):
        return remote(src.at[:, cols(other, g, 1024)], dst.at[core, :, g * 1024 : (g + 1) * 1024],
                      row_send.at[g, n], row_recv.at[g, n], partner)

    def kv_copy(g, n, j, p):
        src = (k_in, v_in)[n]
        chunk = (BACK - j) * 2 + core
        return remote(src.at[:, cols(p, g, 128)],
                      kv.at[g, n, pl.ds(pl.multiple_of(chunk * 128, 128), 128)],
                      kv_send.at[g, n, j, p], kv_recv.at[g, n, j, core], at(j, p))

    def kv_arrived(g, n, j, q):
        dst = kv.at[g, n, ((BACK - j) * 2 + q) * 128 : ((BACK - j) * 2 + q + 1) * 128]
        remote(dst, dst, kv_send.at[g, n, j, q], kv_recv.at[g, n, j, q], partner).wait_recv()

    sends = []
    for g in range(2):
        for n, (src, dst) in enumerate(((q_in, qv), (g_in, gv))):
            sends.append(row_copy(g, n, src, dst))
        for n in range(2):
            sends.append(kv_copy(g, n, 0, other))
            for j in (1, 3, 2, 4):
                for p in range(2):
                    sends.append(kv_copy(g, n, j, p))
    for copy in sends:
        copy.start()

    prep_masks(c // 2 * 256, bounds, ka, qa)
    vt[0, 128:144, :] = jnp.ones((16, 1280), BF)
    vt[1, 128:144, :] = jnp.ones((16, 1280), BF)

    def part_copy(g, kc):
        j, q = BACK - kc // 2, kc % 2
        return remote(part.at[g, kc], got.at[g, j, core], part_send.at[g, kc],
                      part_recv.at[g, j, core], at(-j, q))

    def out_copies(g, n, src, dst):
        here = pltpu.make_async_copy(
            src.at[core, :, g * 1024 : (g + 1) * 1024], dst.at[:, cols(core, g, 1024)],
            out_own_sem.at[g, n])
        there = remote(src.at[other, :, g * 1024 : (g + 1) * 1024], dst.at[:, cols(core, g, 1024)],
                       out_send.at[g, n], out_recv.at[g, n], partner)
        return here, there

    outs = []
    for g in range(2):
        for copy in own[g * 4 : g * 4 + 4]:
            copy.wait()
        for n, (src, dst) in enumerate(((q_in, qv), (g_in, gv))):
            row = dst.at[other, :, g * 1024 : (g + 1) * 1024]
            remote(row, row, row_send.at[g, n], row_recv.at[g, n], partner).wait_recv()
        for n in range(2):
            dst = kv.at[g, n, pl.ds(pl.multiple_of(1024 + other * 128, 128), 128)]
            remote(dst, dst, kv_send.at[g, n, 0, other], kv_recv.at[g, n, 0, other], partner).wait_recv()
            for j in range(1, BACK + 1):
                for q in range(2):
                    kv_arrived(g, n, j, q)
        prep_transposed(g, kv, kt, vt)
        forward(g, qv, gv, kv, ka, qa, vt, s, e, gs, dd, ov)
        outs += out_copies(g, 0, ov, o_out)
        outs[-1].start()
        outs[-2].start()
        for kc in range(8):
            key_grads(g, kc, qv, kv, e, gs, dd, part)
            part_copy(g, kc).start()
        key_grads(g, 8, qv, kv, e, gs, dd, part)
        key_grads(g, 9, qv, kv, e, gs, dd, part)
        remote(part.at[g, 8 + other], got.at[g, 0, core], part_send.at[g, 8],
               part_recv.at[g, 0, core], partner).start()
        for i in range(8):
            query_grads(g, i, kt, e, dqv)
        outs += out_copies(g, 1, dqv, dq_out)
        outs[-1].start()
        outs[-2].start()

    for g in range(2):
        for j in range(1, BACK + 1):
            for p in range(2):
                dst = got.at[g, j, p]
                remote(dst, dst, part_send.at[g, j], part_recv.at[g, j, p], partner).wait_recv()
        dst = got.at[g, 0, other]
        remote(dst, dst, part_send.at[g, 8], part_recv.at[g, 0, other], partner).wait_recv()
        got[g, 0, core] = part[g, 8 + core]
        for p in range(2):
            for n, out in enumerate((dk_out, dv_out)):
                total = got[g, 0, p, n].astype(F32)
                for j in range(1, BACK + 1):
                    total = total + got[g, j, p, n].astype(F32)
                out[:, (2 * p + g) * 128 : (2 * p + g + 1) * 128] = total.astype(BF)

    for copy in sends:
        copy.wait_send()
    for g in range(2):
        for kc in range(8):
            part_copy(g, kc).wait_send()
        remote(part.at[g, 8 + other], got.at[g, 0, core], part_send.at[g, 8],
               part_recv.at[g, 0, core], partner).wait_send()
        for n, (src, dst) in enumerate(((ov, o_out), (dqv, dq_out))):
            here, there = out_copies(g, n, src, dst)
            here.wait()
            there.wait_send()
            arrived = dst.at[:, cols(other, g, 1024)]
            remote(arrived, arrived, out_send.at[g, n], out_recv.at[g, n], partner).wait_recv()


def body(query_rows, key_rows, value_rows, grad_out, doc_bounds):
    hbm = pl.BlockSpec(memory_space=pl.ANY)
    vmem = pl.BlockSpec(memory_space=pltpu.VMEM)
    rows = jax.ShapeDtypeStruct((128, 4096), BF)
    small = jax.ShapeDtypeStruct((128, 512), BF)
    dma = pltpu.SemaphoreType.DMA
    return pl.pallas_call(
        kernel,
        out_shape=(rows, rows, small, small),
        in_specs=[pl.BlockSpec(memory_space=pltpu.SMEM), hbm, hbm, hbm, hbm],
        out_specs=(hbm, hbm, vmem, vmem),
        scratch_shapes=[
            pltpu.VMEM((2, 128, 2048), BF),
            pltpu.VMEM((2, 128, 2048), BF),
            pltpu.VMEM((2, 2, 1280, 128), BF),
            pltpu.VMEM((1280, 128), BF),
            pltpu.VMEM((2, 256, 128), BF),
            pltpu.VMEM((2, 128, 1280), BF),
            pltpu.VMEM((2, 144, 1280), BF),
            pltpu.VMEM((SLOTS, 1152, 256), F32),
            pltpu.VMEM((8, 1152, 256), BF),
            pltpu.VMEM((8, 256, 128), BF),
            pltpu.VMEM((8, 8, 256), F32),
            pltpu.VMEM((2, 128, 2048), BF),
            pltpu.VMEM((2, 128, 2048), BF),
            pltpu.VMEM((2, 10, 2, 128, 128), BF),
            pltpu.VMEM((2, BACK + 1, 2, 2, 128, 128), BF),
            dma((2, 2)), dma((2, 2)), dma((2, 2)), dma((2, 2)),
            dma((2, 2, BACK + 1, 2)), dma((2, 2, BACK + 1, 2)),
            dma((2, 9)), dma((2, BACK + 1, 2)),
            dma((2, 2)), dma((2, 2)), dma((2, 2)),
        ],
        compiler_params=pltpu.CompilerParams(
            collective_id=0, has_side_effects=True, vmem_limit_bytes=56 << 20
        ),
        name="packed_attention",
    )(doc_bounds, query_rows, key_rows, value_rows, grad_out)


def solution(mesh):
    rows = P(("dp", "context"), None)
    return jax.shard_map(
        body,
        mesh=mesh,
        in_specs=(rows, rows, rows, rows, P("dp")),
        out_specs=(rows, rows, rows, rows),
        check_vma=False,
    )
```

```python
import functools

import jax
import jax.numpy as jnp
from jax import lax
from jax.experimental import pallas as pl
from jax.experimental.pallas import tpu as pltpu
from jax.sharding import PartitionSpec as P

BF = jnp.bfloat16
F32 = jnp.float32
MESH = pl.DeviceIdType.MESH
MASKED = -1e30
SCALE = 128 ** -0.5
SCALE2 = SCALE * 1.4426950408889634
SLOTS = 3
CHIPS = 16
PAIRS = (2, 0, 3, 1, 4)
BACK = 4


def nt(a, b):
    return lax.dot_general(a, b, (((1,), (1,)), ((), ())), preferred_element_type=F32)


def nn(a, b):
    return jnp.dot(a, b, preferred_element_type=F32)


def in_doc(pos0, bounds):
    pos = lax.broadcasted_iota(jnp.int32, (128, 128), 0) + pos0
    lane = lax.broadcasted_iota(jnp.int32, (128, 128), 1)
    hit = jnp.zeros((128, 128), F32)
    for t in range(8):
        inside = (pos >= bounds[t]) & (pos < bounds[t + 1]) & (lane == t)
        hit = jnp.where(inside, 1.0, hit)
    return hit, lane < 8


def prep_masks(q0, bounds, ka, qa):
    for a in range(2):
        hit, _ = in_doc(q0 + a * 128, bounds)
        qa[a, 0:128, :] = hit.astype(BF)
        qa[a, 128:256, :] = hit.astype(BF)
    for j in range(10):
        hit, lanes = in_doc(q0 - 1024 + j * 128, bounds)
        ka[j * 128 : (j + 1) * 128, :] = jnp.where(lanes, (1.0 - hit) * MASKED, 0.0).astype(BF)


def prep_transposed(g, n, kv, out):
    for j in range(10):
        r = slice(j * 128, (j + 1) * 128)
        out[g, 0:128, r] = kv[g, n, r, :].T


def prep_rows(g, qv, qr):
    for a in range(2):
        for h in range(8):
            r = a * 1024 + h * 128
            qr[g, r : r + 128, :] = qv[a, :, (g * 8 + h) * 128 : (g * 8 + h + 1) * 128]


def pair(ref, a, h):
    return jnp.concatenate(
        [ref[a, :, h * 128 : h * 128 + 128], ref[a, :, h * 128 + 128 : h * 128 + 256]], axis=0
    )


def window(i):
    return slice(i // 4 * 128, i // 4 * 128 + 1152)


def scores(g, i, qr, kv, ka, qa, s):
    w = window(i)
    q = jnp.concatenate([qr[g, i * 256 : (i + 1) * 256, :], qa[i // 4]], axis=1)
    sc = nt(jnp.concatenate([kv[g, 0, w, :], ka[w, :]], axis=1), q)
    key = lax.broadcasted_iota(jnp.int32, (128, 256), 0)
    query = lax.broadcasted_iota(jnp.int32, (128, 256), 1) % 128
    last = jnp.where(key <= query, sc[1024:], MASKED)
    sc = jnp.concatenate([sc[:1024], last], axis=0)
    s[i % SLOTS] = sc
    m = jnp.max(sc.reshape(144, 8, 256), axis=0)
    return jnp.max(m, axis=0, keepdims=True) * SCALE2


def exps(i, m, s, e):
    e[window(i), i * 256 : (i + 1) * 256] = jnp.exp2(s[i % SLOTS] * SCALE2 - m).astype(BF)


def attend(g, i, vt, e):
    return nn(vt[g, :, window(i)], e[window(i), i * 256 : (i + 1) * 256])


def finish(g, i, ot, gv, gs, ov):
    a, h = i // 4, g * 8 + i % 4 * 2
    o = ot[0:128].T
    linv = 1.0 / ot[128:136].T[:, 0:1]
    o = o * linv
    gp = (pair(gv, a, h).astype(F32) * linv).astype(BF)
    r = slice(i * 256, (i + 1) * 256)
    gs[r, 0:128] = gp
    gs[r, 128:256] = (-(gp.astype(F32) * o)).astype(BF)
    ob = o.astype(BF)
    ov[a, :, h * 128 : h * 128 + 128] = ob[0:128]
    ov[a, :, h * 128 + 128 : h * 128 + 256] = ob[128:256]


def forward(g, qr, gv, kv, ka, qa, vt, s, e, gs, ov, beside):
    m, ot = {}, {}
    for t in range(11):
        beside(t)
        if t < 8:
            m[t] = scores(g, t, qr, kv, ka, qa, s)
        if 1 <= t < 9:
            exps(t - 1, m[t - 1], s, e)
        if 2 <= t < 10:
            ot[t - 2] = attend(g, t - 2, vt, e)
        if 3 <= t:
            finish(g, t - 3, ot[t - 3], gv, gs, ov)


def score_grads(g, pr, kv, e, gs, ds):
    values = jnp.concatenate(
        [kv[g, 1, pr * 256 : (pr + 1) * 256, :], jnp.ones((256, 128), BF)], axis=1
    )
    for i in range(8):
        lo = 128 if i >= 4 and pr == 0 else 0
        hi = 128 if i < 4 and pr == 4 else 256
        r, c = slice(pr * 256 + lo, pr * 256 + hi), slice(i * 256, (i + 1) * 256)
        dp = nt(values[lo:hi], gs[c, :])
        ds[r, c] = e[r, c] * dp.astype(BF)


def over_queries(pr, left, right):
    r = pr * 256
    if pr == 0:
        return (nn(left[0:128, 0:1024], right(0, 1024)), nn(left[128:256, :], right(0, 2048)))
    if pr == 4:
        return (nn(left[r : r + 128, :], right(0, 2048)),
                nn(left[r + 128 : r + 256, 1024:2048], right(1024, 2048)))
    x = nn(left[r : r + 256, :], right(0, 2048))
    return x[0:128], x[128:256]


def key_grads(g, pr, qr, e, gs, ds, part):
    dv = over_queries(pr, e, lambda x0, x1: gs[x0:x1, 0:128])
    dk = over_queries(pr, ds, lambda x0, x1: qr[g, x0:x1, :])
    for n in range(2):
        part[g, pr * 2 + n, 0] = (dk[n] * SCALE).astype(BF)
        part[g, pr * 2 + n, 1] = dv[n].astype(BF)


def query_grads(g, i, kt, ds, dqv):
    a, h = i // 4, g * 8 + i % 4 * 2
    dq = (nn(kt[g, :, window(i)], ds[window(i), i * 256 : (i + 1) * 256]) * SCALE).T.astype(BF)
    dqv[a, :, h * 128 : h * 128 + 128] = dq[0:128]
    dqv[a, :, h * 128 + 128 : h * 128 + 256] = dq[128:256]


def kernel(
    bounds, q_in, k_in, v_in, g_in,
    o_out, dq_out, dk_out, dv_out,
    qv, gv, kv, ka, qa, qr, kt, vt, s, e, ds, gs, ov, dqv, part, got,
    own_sem, kv_own_sem, row_send, row_recv, kv_send, kv_recv, part_send, part_recv,
    out_own_sem, out_send, out_recv,
):
    dp = lax.axis_index("dp")
    c = lax.axis_index("context")
    chip, core = c // 2, c % 2
    other = 1 - core
    partner = chip * 2 + other

    def at(step, p):
        return lax.rem(chip + step + CHIPS, CHIPS) * 2 + p

    def cols(p, g, width):
        return pl.ds(pl.multiple_of(p * (2 * width) + g * width, width), width)

    def remote(src, dst, send, recv, to):
        return pltpu.make_async_remote_copy(
            src_ref=src, dst_ref=dst, send_sem=send, recv_sem=recv,
            device_id=(dp, to), device_id_type=MESH,
        )

    barrier = pltpu.get_barrier_semaphore()
    peers = [partner]
    for j in range(1, BACK + 1):
        for p in range(2):
            peers += [at(j, p), at(-j, p)]
    for peer in peers:
        pl.semaphore_signal(barrier, inc=1, device_id=(dp, peer), device_id_type=MESH)

    own = []
    for g in range(2):
        for n, (src, dst) in enumerate(((q_in, qv), (g_in, gv))):
            own.append(pltpu.make_async_copy(
                src.at[:, cols(core, g, 1024)], dst.at[core, :, g * 1024 : (g + 1) * 1024],
                own_sem.at[g, n]))
        for n, src in enumerate((k_in, v_in)):
            own.append(pltpu.make_async_copy(
                src.at[:, cols(core, g, 128)],
                kv.at[g, n, pl.ds(pl.multiple_of(1024 + core * 128, 128), 128)],
                kv_own_sem.at[g, n]))
    for copy in own:
        copy.start()
    pl.semaphore_wait(barrier, len(peers))

    def row_copy(g, n, src, dst):
        return remote(src.at[:, cols(other, g, 1024)], dst.at[core, :, g * 1024 : (g + 1) * 1024],
                      row_send.at[g, n], row_recv.at[g, n], partner)

    def kv_copy(g, n, j, p):
        src = (k_in, v_in)[n]
        chunk = (BACK - j) * 2 + core
        return remote(src.at[:, cols(p, g, 128)],
                      kv.at[g, n, pl.ds(pl.multiple_of(chunk * 128, 128), 128)],
                      kv_send.at[g, n, j, p], kv_recv.at[g, n, j, core], at(j, p))

    def kv_arrived(g, n, j, q):
        dst = kv.at[g, n, ((BACK - j) * 2 + q) * 128 : ((BACK - j) * 2 + q + 1) * 128]
        remote(dst, dst, kv_send.at[g, n, j, q], kv_recv.at[g, n, j, q], partner).wait_recv()

    sends = [[], []]
    for g in range(2):
        for n, (src, dst) in enumerate(((q_in, qv), (g_in, gv))):
            sends[g].append(row_copy(g, n, src, dst))
        for n in range(2):
            sends[g].append(kv_copy(g, n, 0, other))
            for j in (1, 3, 4):
                for p in range(2):
                    sends[g].append(kv_copy(g, n, j, p))
    for copy in sends[0]:
        copy.start()

    prep_masks(c // 2 * 256, bounds, ka, qa)
    vt[0, 128:144, :] = jnp.ones((16, 1280), BF)
    vt[1, 128:144, :] = jnp.ones((16, 1280), BF)
    def relay(g, n, way):
        src, dst, to = ((6, 4, 1), (3, 5, -1))[way]
        return remote(kv.at[g, n, src * 128 : (src + 1) * 128], kv.at[g, n, dst * 128 : (dst + 1) * 128],
                      kv_send.at[g, n, 2, way], kv_recv.at[g, n, 2, way], at(to, core))

    def relay_when_here(g, n):
        kv_arrived(g, n, 1, 0)
        relay(g, n, 0).start()
        kv_arrived(g, n, 3, 1)
        relay(g, n, 1).start()

    relay_when_here(0, 0)
    relay_when_here(0, 1)
    for copy in sends[1]:
        copy.start()

    def part_copy(g, kc):
        if kc in (4, 5):
            to, way = ((-1, 0), (1, 1))[kc - 4]
            return remote(part.at[g, kc], got.at[g, 2, way], part_send.at[g, kc],
                          part_recv.at[g, 2, way], at(to, core))
        j, q = BACK - kc // 2, kc % 2
        return remote(part.at[g, kc], got.at[g, j, core], part_send.at[g, kc],
                      part_recv.at[g, j, core], at(-j, q))

    def part_join(g, way):
        kc = (6, 3)[way]
        dst = got.at[g, 2, way]
        remote(dst, dst, part_send.at[g, kc], part_recv.at[g, 2, way], partner).wait_recv()
        part[g, kc] = (part[g, kc].astype(F32) + got[g, 2, way].astype(F32)).astype(BF)
        part_copy(g, kc).start()

    def out_copies(g, n, src, dst):
        here = pltpu.make_async_copy(
            src.at[core, :, g * 1024 : (g + 1) * 1024], dst.at[:, cols(core, g, 1024)],
            out_own_sem.at[g, n])
        there = remote(src.at[other, :, g * 1024 : (g + 1) * 1024], dst.at[:, cols(core, g, 1024)],
                       out_send.at[g, n], out_recv.at[g, n], partner)
        return here, there

    outs = []
    for g in range(2):
        for copy in own[g * 4 : g * 4 + 4]:
            copy.wait()
        for n, (src, dst) in enumerate(((q_in, qv), (g_in, gv))):
            row = dst.at[other, :, g * 1024 : (g + 1) * 1024]
            remote(row, row, row_send.at[g, n], row_recv.at[g, n], partner).wait_recv()
        prep_rows(g, qv, qr)
        for n in range(2):
            dst = kv.at[g, n, pl.ds(pl.multiple_of(1024 + other * 128, 128), 128)]
            remote(dst, dst, kv_send.at[g, n, 0, other], kv_recv.at[g, n, 0, other], partner).wait_recv()
            for j in range(1, BACK + 1):
                for q in range(2):
                    if (j, q) not in ((1, 0), (3, 1)):
                        kv_arrived(g, n, j, q)
            prep_transposed(g, n, kv, (kt, vt)[n])

        def beside(t):
            if g == 0 and t in (8, 10):
                relay_when_here(1, (t - 8) // 2)
            if g == 1 and t in (3, 4):
                part_join(0, t - 3)

        forward(g, qr, gv, kv, ka, qa, vt, s, e, gs, ov, beside)
        outs += out_copies(g, 0, ov, o_out)
        outs[-1].start()
        outs[-2].start()
        for n in range(len(PAIRS) + 1):
            if n < len(PAIRS):
                score_grads(g, PAIRS[n], kv, e, gs, ds)
            if n > 0:
                pr = PAIRS[n - 1]
                key_grads(g, pr, qr, e, gs, ds, part)
                if pr < BACK:
                    for kc in (2 * pr, 2 * pr + 1):
                        if kc not in (3, 6):
                            part_copy(g, kc).start()
                else:
                    remote(part.at[g, 8 + other], got.at[g, 0, core], part_send.at[g, 8],
                           part_recv.at[g, 0, core], partner).start()
        for i in range(8):
            query_grads(g, i, kt, ds, dqv)
        outs += out_copies(g, 1, dqv, dq_out)
        outs[-1].start()
        outs[-2].start()

    part_join(1, 0)
    part_join(1, 1)
    for g in range(2):
        for j in (1, 3, 4):
            for p in range(2):
                dst = got.at[g, j, p]
                remote(dst, dst, part_send.at[g, j], part_recv.at[g, j, p], partner).wait_recv()
        dst = got.at[g, 0, other]
        remote(dst, dst, part_send.at[g, 8], part_recv.at[g, 0, other], partner).wait_recv()
        got[g, 0, core] = part[g, 8 + core]
        for p in range(2):
            for n, out in enumerate((dk_out, dv_out)):
                total = got[g, 0, p, n].astype(F32)
                for j in (1, 3, 4):
                    total = total + got[g, j, p, n].astype(F32)
                out[:, (2 * p + g) * 128 : (2 * p + g + 1) * 128] = total.astype(BF)

    for copy in sends[0] + sends[1]:
        copy.wait_send()
    for g in range(2):
        for n in range(2):
            for way in range(2):
                relay(g, n, way).wait_send()
    for g in range(2):
        for kc in range(8):
            part_copy(g, kc).wait_send()
        remote(part.at[g, 8 + other], got.at[g, 0, core], part_send.at[g, 8],
               part_recv.at[g, 0, core], partner).wait_send()
        for n, (src, dst) in enumerate(((ov, o_out), (dqv, dq_out))):
            here, there = out_copies(g, n, src, dst)
            here.wait()
            there.wait_send()
            arrived = dst.at[:, cols(other, g, 1024)]
            remote(arrived, arrived, out_send.at[g, n], out_recv.at[g, n], partner).wait_recv()


def hand_over(*refs):
    src, dst, held, sems = refs[:4], refs[4:8], refs[8:12], refs[12]
    way_in, way_out = [], []
    for n in range(4):
        pieces = 4 if n < 2 else 1
        rows = src[n].shape[0] // pieces
        for m in range(pieces):
            r = pl.ds(m * rows, rows)
            way_in.append(pltpu.make_async_copy(src[n].at[r], held[n].at[r], sems.at[0, n, m]))
            way_out.append(pltpu.make_async_copy(held[n].at[r], dst[n].at[r], sems.at[1, n, m]))
    for copy in way_in:
        copy.start()
    for here, there in zip(way_in, way_out):
        here.wait()
        there.start()
    for copy in way_out:
        copy.wait()


def body(query_rows, key_rows, value_rows, grad_out, doc_bounds):
    hbm = pl.BlockSpec(memory_space=pl.ANY)
    vmem = pl.BlockSpec(memory_space=pltpu.VMEM)
    rows = jax.ShapeDtypeStruct((128, 4096), BF)
    small = jax.ShapeDtypeStruct((128, 512), BF)
    dma = pltpu.SemaphoreType.DMA
    results = pl.pallas_call(
        kernel,
        out_shape=(rows, rows, small, small),
        in_specs=[pl.BlockSpec(memory_space=pltpu.SMEM), hbm, hbm, hbm, hbm],
        out_specs=(hbm, hbm, vmem, vmem),
        scratch_shapes=[
            pltpu.VMEM((2, 128, 2048), BF),
            pltpu.VMEM((2, 128, 2048), BF),
            pltpu.VMEM((2, 2, 1280, 128), BF),
            pltpu.VMEM((1280, 128), BF),
            pltpu.VMEM((2, 256, 128), BF),
            pltpu.VMEM((2, 2048, 128), BF),
            pltpu.VMEM((2, 128, 1280), BF),
            pltpu.VMEM((2, 144, 1280), BF),
            pltpu.VMEM((SLOTS, 1152, 256), F32),
            pltpu.VMEM((1280, 2048), BF),
            pltpu.VMEM((1280, 2048), BF),
            pltpu.VMEM((2048, 256), BF),
            pltpu.VMEM((2, 128, 2048), BF),
            pltpu.VMEM((2, 128, 2048), BF),
            pltpu.VMEM((2, 10, 2, 128, 128), BF),
            pltpu.VMEM((2, BACK + 1, 2, 2, 128, 128), BF),
            dma((2, 2)), dma((2, 2)), dma((2, 2)), dma((2, 2)),
            dma((2, 2, BACK + 1, 2)), dma((2, 2, BACK + 1, 2)),
            dma((2, 9)), dma((2, BACK + 1, 2)),
            dma((2, 2)), dma((2, 2)), dma((2, 2)),
        ],
        compiler_params=pltpu.CompilerParams(
            collective_id=0, has_side_effects=True, vmem_limit_bytes=56 << 20
        ),
        name="packed_attention",
    )(doc_bounds, query_rows, key_rows, value_rows, grad_out)
    return pl.pallas_call(
        hand_over,
        out_shape=(rows, rows, small, small),
        in_specs=[hbm] * 4,
        out_specs=[hbm] * 4,
        scratch_shapes=[pltpu.VMEM(x.shape, BF) for x in (rows, rows, small, small)] + [dma((2, 4, 4))],
        name="hand_over",
    )(*results)


def solution(mesh):
    rows = P(("dp", "context"), None)
    return jax.shard_map(
        body,
        mesh=mesh,
        in_specs=(rows, rows, rows, rows, P("dp")),
        out_specs=(rows, rows, rows, rows),
        check_vma=False,
    )
```

```python
import functools

import jax
import jax.numpy as jnp
from jax import lax
from jax.experimental import pallas as pl
from jax.experimental.pallas import tpu as pltpu
from jax.sharding import PartitionSpec as P

BF = jnp.bfloat16
F32 = jnp.float32
MESH = pl.DeviceIdType.MESH
MASKED = -1e30
SCALE = 128 ** -0.5
SCALE2 = SCALE * 1.4426950408889634
SLOTS = 3
CHIPS = 16
PAIRS = (2, 0, 3, 1, 4)
BACK = 4


def nt(a, b):
    return lax.dot_general(a, b, (((1,), (1,)), ((), ())), preferred_element_type=F32)


def nn(a, b):
    return jnp.dot(a, b, preferred_element_type=F32)


def in_doc(pos0, bounds):
    pos = lax.broadcasted_iota(jnp.int32, (128, 128), 0) + pos0
    lane = lax.broadcasted_iota(jnp.int32, (128, 128), 1)
    hit = jnp.zeros((128, 128), F32)
    for t in range(8):
        inside = (pos >= bounds[t]) & (pos < bounds[t + 1]) & (lane == t)
        hit = jnp.where(inside, 1.0, hit)
    return hit, lane < 8


def prep_masks(q0, bounds, ka, qa):
    for a in range(2):
        hit, _ = in_doc(q0 + a * 128, bounds)
        qa[a, 0:128, :] = hit.astype(BF)
        qa[a, 128:256, :] = hit.astype(BF)
    for j in range(10):
        hit, lanes = in_doc(q0 - 1024 + j * 128, bounds)
        ka[j * 128 : (j + 1) * 128, :] = jnp.where(lanes, (1.0 - hit) * MASKED, 0.0).astype(BF)


def prep_transposed(g, n, kv, out):
    for j in range(10):
        r = slice(j * 128, (j + 1) * 128)
        out[g, 0:128, r] = kv[g, n, r, :].T


def prep_rows(g, qv, qr):
    for a in range(2):
        for h in range(8):
            r = a * 1024 + h * 128
            qr[g, r : r + 128, :] = qv[a, :, (g * 8 + h) * 128 : (g * 8 + h + 1) * 128]


def pair(ref, a, h):
    return jnp.concatenate(
        [ref[a, :, h * 128 : h * 128 + 128], ref[a, :, h * 128 + 128 : h * 128 + 256]], axis=0
    )


def window(i):
    return slice(i // 4 * 128, i // 4 * 128 + 1152)


def scores(g, i, qr, kv, ka, qa, s):
    w = window(i)
    q = jnp.concatenate([qr[g, i * 256 : (i + 1) * 256, :], qa[i // 4]], axis=1)
    sc = nt(jnp.concatenate([kv[g, 0, w, :], ka[w, :]], axis=1), q)
    key = lax.broadcasted_iota(jnp.int32, (128, 256), 0)
    query = lax.broadcasted_iota(jnp.int32, (128, 256), 1) % 128
    last = jnp.where(key <= query, sc[1024:], MASKED)
    sc = jnp.concatenate([sc[:1024], last], axis=0)
    s[i % SLOTS] = sc
    m = jnp.max(sc.reshape(144, 8, 256), axis=0)
    return jnp.max(m, axis=0, keepdims=True) * SCALE2


def exps(i, m, s, e):
    e[window(i), i * 256 : (i + 1) * 256] = jnp.exp2(s[i % SLOTS] * SCALE2 - m).astype(BF)


def attend(g, i, vt, e):
    return nn(vt[g, :, window(i)], e[window(i), i * 256 : (i + 1) * 256])


def finish(g, i, ot, gv, gs, ov):
    a, h = i // 4, g * 8 + i % 4 * 2
    o = ot[0:128].T
    linv = 1.0 / ot[128:136].T[:, 0:1]
    o = o * linv
    gp = (pair(gv, a, h).astype(F32) * linv).astype(BF)
    r = slice(i * 256, (i + 1) * 256)
    gs[r, 0:128] = gp
    gs[r, 128:256] = (-(gp.astype(F32) * o)).astype(BF)
    ob = o.astype(BF)
    ov[a, :, h * 128 : h * 128 + 128] = ob[0:128]
    ov[a, :, h * 128 + 128 : h * 128 + 256] = ob[128:256]


def forward(g, qr, gv, kv, ka, qa, vt, s, e, gs, ov, beside):
    m, ot = {}, {}
    for t in range(11):
        beside(t)
        if t < 8:
            m[t] = scores(g, t, qr, kv, ka, qa, s)
        if 1 <= t < 9:
            exps(t - 1, m[t - 1], s, e)
        if 2 <= t < 10:
            ot[t - 2] = attend(g, t - 2, vt, e)
        if 3 <= t:
            finish(g, t - 3, ot[t - 3], gv, gs, ov)


def score_grads(g, pr, kv, e, gs, ds):
    values = jnp.concatenate(
        [kv[g, 1, pr * 256 : (pr + 1) * 256, :], jnp.ones((256, 128), BF)], axis=1
    )
    for i in range(8):
        lo = 128 if i >= 4 and pr == 0 else 0
        hi = 128 if i < 4 and pr == 4 else 256
        r, c = slice(pr * 256 + lo, pr * 256 + hi), slice(i * 256, (i + 1) * 256)
        dp = nt(values[lo:hi], gs[c, :])
        ds[r, c] = e[r, c] * dp.astype(BF)


def over_queries(pr, left, right):
    r = pr * 256
    if pr == 0:
        return (nn(left[0:128, 0:1024], right(0, 1024)), nn(left[128:256, :], right(0, 2048)))
    if pr == 4:
        return (nn(left[r : r + 128, :], right(0, 2048)),
                nn(left[r + 128 : r + 256, 1024:2048], right(1024, 2048)))
    x = nn(left[r : r + 256, :], right(0, 2048))
    return x[0:128], x[128:256]


def key_grads(g, pr, qr, e, gs, ds, part):
    dv = over_queries(pr, e, lambda x0, x1: gs[x0:x1, 0:128])
    dk = over_queries(pr, ds, lambda x0, x1: qr[g, x0:x1, :])
    for n in range(2):
        part[g, pr * 2 + n, 0] = (dk[n] * SCALE).astype(BF)
        part[g, pr * 2 + n, 1] = dv[n].astype(BF)


def query_grads(g, i, kt, ds, dqv):
    a, h = i // 4, g * 8 + i % 4 * 2
    dq = (nn(kt[g, :, window(i)], ds[window(i), i * 256 : (i + 1) * 256]) * SCALE).T.astype(BF)
    dqv[a, :, h * 128 : h * 128 + 128] = dq[0:128]
    dqv[a, :, h * 128 + 128 : h * 128 + 256] = dq[128:256]


def kernel(
    bounds, q_in, k_in, v_in, g_in,
    o_out, dq_out, dk_out, dv_out,
    qv, gv, kv, ka, qa, qr, kt, vt, s, e, ds, gs, ov, dqv, part, got,
    own_sem, kv_own_sem, row_send, row_recv, kv_send, kv_recv, part_send, part_recv,
    out_own_sem, out_send, out_recv,
):
    dp = lax.axis_index("dp")
    c = lax.axis_index("context")
    chip, core = c // 2, c % 2
    other = 1 - core
    partner = chip * 2 + other

    def at(step, p):
        return lax.rem(chip + step + CHIPS, CHIPS) * 2 + p

    def cols(p, g, width):
        return pl.ds(pl.multiple_of(p * (2 * width) + g * width, width), width)

    def remote(src, dst, send, recv, to):
        return pltpu.make_async_remote_copy(
            src_ref=src, dst_ref=dst, send_sem=send, recv_sem=recv,
            device_id=(dp, to), device_id_type=MESH,
        )

    barrier = pltpu.get_barrier_semaphore()
    peers = [partner]
    for j in range(1, BACK + 1):
        for p in range(2):
            peers += [at(j, p), at(-j, p)]
    for peer in peers:
        pl.semaphore_signal(barrier, inc=1, device_id=(dp, peer), device_id_type=MESH)

    own = []
    for g in range(2):
        for n, (src, dst) in enumerate(((q_in, qv), (g_in, gv))):
            own.append(pltpu.make_async_copy(
                src.at[:, cols(core, g, 1024)], dst.at[core, :, g * 1024 : (g + 1) * 1024],
                own_sem.at[g, n]))
        for n, src in enumerate((k_in, v_in)):
            own.append(pltpu.make_async_copy(
                src.at[:, cols(core, g, 128)],
                kv.at[g, n, pl.ds(pl.multiple_of(1024 + core * 128, 128), 128)],
                kv_own_sem.at[g, n]))
    for copy in own:
        copy.start()
    pl.semaphore_wait(barrier, len(peers))

    def row_copy(g, n, src, dst):
        return remote(src.at[:, cols(other, g, 1024)], dst.at[core, :, g * 1024 : (g + 1) * 1024],
                      row_send.at[g, n], row_recv.at[g, n], partner)

    def kv_copy(g, n, j, p):
        src = (k_in, v_in)[n]
        chunk = (BACK - j) * 2 + core
        return remote(src.at[:, cols(p, g, 128)],
                      kv.at[g, n, pl.ds(pl.multiple_of(chunk * 128, 128), 128)],
                      kv_send.at[g, n, j, p], kv_recv.at[g, n, j, core], at(j, p))

    def kv_arrived(g, n, j, q):
        dst = kv.at[g, n, ((BACK - j) * 2 + q) * 128 : ((BACK - j) * 2 + q + 1) * 128]
        remote(dst, dst, kv_send.at[g, n, j, q], kv_recv.at[g, n, j, q], partner).wait_recv()

    sends = [[], []]
    for g in range(2):
        for n, (src, dst) in enumerate(((q_in, qv), (g_in, gv))):
            sends[g].append(row_copy(g, n, src, dst))
        for n in range(2):
            sends[g].append(kv_copy(g, n, 0, other))
            for j in (1, 3, 4):
                for p in range(2):
                    sends[g].append(kv_copy(g, n, j, p))
    for copy in sends[0]:
        copy.start()

    prep_masks(c // 2 * 256, bounds, ka, qa)
    vt[0, 128:144, :] = jnp.ones((16, 1280), BF)
    vt[1, 128:144, :] = jnp.ones((16, 1280), BF)
    def relay(g, n, way):
        src, dst, to = ((6, 4, 1), (3, 5, -1))[way]
        return remote(kv.at[g, n, src * 128 : (src + 1) * 128], kv.at[g, n, dst * 128 : (dst + 1) * 128],
                      kv_send.at[g, n, 2, way], kv_recv.at[g, n, 2, way], at(to, core))

    def relay_when_here(g, n, way):
        kv_arrived(g, n, (1, 3)[way], way)
        relay(g, n, way).start()

    for n in range(2):
        for way in range(2):
            relay_when_here(0, n, way)
    for copy in sends[1]:
        copy.start()

    def part_copy(g, kc):
        if kc in (4, 5):
            to, way = ((-1, 0), (1, 1))[kc - 4]
            return remote(part.at[g, kc], got.at[g, 2, way], part_send.at[g, kc],
                          part_recv.at[g, 2, way], at(to, core))
        j, q = BACK - kc // 2, kc % 2
        return remote(part.at[g, kc], got.at[g, j, core], part_send.at[g, kc],
                      part_recv.at[g, j, core], at(-j, q))

    def part_join(g, way):
        kc = (6, 3)[way]
        dst = got.at[g, 2, way]
        remote(dst, dst, part_send.at[g, kc], part_recv.at[g, 2, way], partner).wait_recv()
        part[g, kc] = (part[g, kc].astype(F32) + got[g, 2, way].astype(F32)).astype(BF)
        part_copy(g, kc).start()

    def out_copies(g, n, src, dst):
        here = pltpu.make_async_copy(
            src.at[core, :, g * 1024 : (g + 1) * 1024], dst.at[:, cols(core, g, 1024)],
            out_own_sem.at[g, n])
        there = remote(src.at[other, :, g * 1024 : (g + 1) * 1024], dst.at[:, cols(core, g, 1024)],
                       out_send.at[g, n], out_recv.at[g, n], partner)
        return here, there

    outs = []
    for g in range(2):
        for copy in own[g * 4 : g * 4 + 4]:
            copy.wait()
        for n, (src, dst) in enumerate(((q_in, qv), (g_in, gv))):
            row = dst.at[other, :, g * 1024 : (g + 1) * 1024]
            remote(row, row, row_send.at[g, n], row_recv.at[g, n], partner).wait_recv()
        prep_rows(g, qv, qr)
        for n in range(2):
            dst = kv.at[g, n, pl.ds(pl.multiple_of(1024 + other * 128, 128), 128)]
            remote(dst, dst, kv_send.at[g, n, 0, other], kv_recv.at[g, n, 0, other], partner).wait_recv()
            for j in range(1, BACK + 1):
                for q in range(2):
                    if (j, q) not in ((1, 0), (3, 1)):
                        kv_arrived(g, n, j, q)
            prep_transposed(g, n, kv, (kt, vt)[n])

        def beside(t):
            if g == 0 and t in (3, 4, 6, 7):
                relay_when_here(1, t // 6, t % 3)
            if g == 1 and t in (3, 4):
                part_join(0, t - 3)

        forward(g, qr, gv, kv, ka, qa, vt, s, e, gs, ov, beside)
        outs += out_copies(g, 0, ov, o_out)
        outs[-1].start()
        outs[-2].start()
        for n in range(len(PAIRS) + 1):
            if n < len(PAIRS):
                score_grads(g, PAIRS[n], kv, e, gs, ds)
            if n > 0:
                pr = PAIRS[n - 1]
                key_grads(g, pr, qr, e, gs, ds, part)
                if pr < BACK:
                    for kc in (2 * pr, 2 * pr + 1):
                        if kc not in (3, 6):
                            part_copy(g, kc).start()
                else:
                    remote(part.at[g, 8 + other], got.at[g, 0, core], part_send.at[g, 8],
                           part_recv.at[g, 0, core], partner).start()
        for i in range(8):
            query_grads(g, i, kt, ds, dqv)
        outs += out_copies(g, 1, dqv, dq_out)
        outs[-1].start()
        outs[-2].start()

    part_join(1, 0)
    part_join(1, 1)
    for g in range(2):
        for j in (1, 3, 4):
            for p in range(2):
                dst = got.at[g, j, p]
                remote(dst, dst, part_send.at[g, j], part_recv.at[g, j, p], partner).wait_recv()
        dst = got.at[g, 0, other]
        remote(dst, dst, part_send.at[g, 8], part_recv.at[g, 0, other], partner).wait_recv()
        got[g, 0, core] = part[g, 8 + core]
        for p in range(2):
            for n, out in enumerate((dk_out, dv_out)):
                total = got[g, 0, p, n].astype(F32)
                for j in (1, 3, 4):
                    total = total + got[g, j, p, n].astype(F32)
                out[:, (2 * p + g) * 128 : (2 * p + g + 1) * 128] = total.astype(BF)

    for copy in sends[0] + sends[1]:
        copy.wait_send()
    for g in range(2):
        for n in range(2):
            for way in range(2):
                relay(g, n, way).wait_send()
    for g in range(2):
        for kc in range(8):
            part_copy(g, kc).wait_send()
        remote(part.at[g, 8 + other], got.at[g, 0, core], part_send.at[g, 8],
               part_recv.at[g, 0, core], partner).wait_send()
        for n, (src, dst) in enumerate(((ov, o_out), (dqv, dq_out))):
            here, there = out_copies(g, n, src, dst)
            here.wait()
            there.wait_send()
            arrived = dst.at[:, cols(other, g, 1024)]
            remote(arrived, arrived, out_send.at[g, n], out_recv.at[g, n], partner).wait_recv()


def hand_over(*refs):
    src, dst, held, sems = refs[:4], refs[4:8], refs[8:12], refs[12]
    way_in, way_out = [], []
    for n in range(4):
        pieces = 4 if n < 2 else 1
        rows = src[n].shape[0] // pieces
        for m in range(pieces):
            r = pl.ds(m * rows, rows)
            way_in.append(pltpu.make_async_copy(src[n].at[r], held[n].at[r], sems.at[0, n, m]))
            way_out.append(pltpu.make_async_copy(held[n].at[r], dst[n].at[r], sems.at[1, n, m]))
    for copy in way_in:
        copy.start()
    for here, there in zip(way_in, way_out):
        here.wait()
        there.start()
    for copy in way_out:
        copy.wait()


def body(query_rows, key_rows, value_rows, grad_out, doc_bounds):
    hbm = pl.BlockSpec(memory_space=pl.ANY)
    vmem = pl.BlockSpec(memory_space=pltpu.VMEM)
    rows = jax.ShapeDtypeStruct((128, 4096), BF)
    small = jax.ShapeDtypeStruct((128, 512), BF)
    dma = pltpu.SemaphoreType.DMA
    results = pl.pallas_call(
        kernel,
        out_shape=(rows, rows, small, small),
        in_specs=[pl.BlockSpec(memory_space=pltpu.SMEM), hbm, hbm, hbm, hbm],
        out_specs=(hbm, hbm, vmem, vmem),
        scratch_shapes=[
            pltpu.VMEM((2, 128, 2048), BF),
            pltpu.VMEM((2, 128, 2048), BF),
            pltpu.VMEM((2, 2, 1280, 128), BF),
            pltpu.VMEM((1280, 128), BF),
            pltpu.VMEM((2, 256, 128), BF),
            pltpu.VMEM((2, 2048, 128), BF),
            pltpu.VMEM((2, 128, 1280), BF),
            pltpu.VMEM((2, 144, 1280), BF),
            pltpu.VMEM((SLOTS, 1152, 256), F32),
            pltpu.VMEM((1280, 2048), BF),
            pltpu.VMEM((1280, 2048), BF),
            pltpu.VMEM((2048, 256), BF),
            pltpu.VMEM((2, 128, 2048), BF),
            pltpu.VMEM((2, 128, 2048), BF),
            pltpu.VMEM((2, 10, 2, 128, 128), BF),
            pltpu.VMEM((2, BACK + 1, 2, 2, 128, 128), BF),
            dma((2, 2)), dma((2, 2)), dma((2, 2)), dma((2, 2)),
            dma((2, 2, BACK + 1, 2)), dma((2, 2, BACK + 1, 2)),
            dma((2, 9)), dma((2, BACK + 1, 2)),
            dma((2, 2)), dma((2, 2)), dma((2, 2)),
        ],
        compiler_params=pltpu.CompilerParams(
            collective_id=0, has_side_effects=True, vmem_limit_bytes=56 << 20
        ),
        name="packed_attention",
    )(doc_bounds, query_rows, key_rows, value_rows, grad_out)
    return pl.pallas_call(
        hand_over,
        out_shape=(rows, rows, small, small),
        in_specs=[hbm] * 4,
        out_specs=[hbm] * 4,
        scratch_shapes=[pltpu.VMEM(x.shape, BF) for x in (rows, rows, small, small)] + [dma((2, 4, 4))],
        name="hand_over",
    )(*results)


def solution(mesh):
    rows = P(("dp", "context"), None)
    return jax.shard_map(
        body,
        mesh=mesh,
        in_specs=(rows, rows, rows, rows, P("dp")),
        out_specs=(rows, rows, rows, rows),
        check_vma=False,
    )
```
